512 devices in a mesh: gx: 4 (over z_hi), gy: 16 (over y, x), gz: 8 (over z_lo, core).
Axes of the slice: x: 4, y: 4, z: 16 (z_hi: 4, z_lo: 4; z = z_hi * 4 + z_lo), core: 2. Of those that a mesh axis runs over, the one named last changes fastest.
Arguments:
- features: float32 [4, 32, 8, 128, 256], P('gx', 'gy', 'gz'), may hold values from -82 to 82
- occupancy: int32 [4, 32, 8], P('gx', 'gy', 'gz'), may hold values from 1 to 128, as said below
- dest_bin: int32 [4, 32, 8], P('gx', 'gy', 'gz'), may hold values from 0 to 1023, as said below
- query_weight: bfloat16 [256, 256], replicated, may hold values from -0.375 to 0.375
- key_weight: bfloat16 [256, 256], replicated, may hold values from -0.375 to 0.375
- value_weight: bfloat16 [256, 256], replicated, may hold values from -0.375 to 0.375
- out_weight: bfloat16 [256, 256], replicated, may hold values from -0.375 to 0.375
- up_weight: bfloat16 [256, 1024], replicated, may hold values from -0.375 to 0.375
- down_weight: bfloat16 [1024, 256], replicated, may hold values from -0.1875 to 0.1875
- attention_gain: float32 [256], replicated, may hold values from 0.25 to 1.75
- feed_gain: float32 [256], replicated, may hold values from 0.25 to 1.75
Outputs:
- particles: float32 [4, 32, 8, 128, 256], P('gx', 'gy', 'gz')
The draws below stay inside these ranges and needn't reach their ends.
Inputs may be any that keep to these rules, and one draw needn't show every extreme that they name: `occupancy`: some bin holds 128 live particles. `dest_bin`: A permutation of the bins; every block stays on a device with the same gx and gy index, and each device sends at most 1 block to any one device, a bound that some pair of devices reaches.
All inputs are finite; a program needn't handle non-finite values.
Results may differ from the reference program's by a relative error of at most 0.0065.
The reference program's roundings to bfloat16 on the way (of `rows`, `query`, `weights`, `attended` and `inner`) count: a program that leaves them out, or rounds other values in their place, can miss the bound.
Values may be sent and summed in bfloat16 or wider, within the bound.
A program may use at most 64 MiB of HBM per device.

```python
import jax
import jax.numpy as jnp
from jax import lax

W = 256
HEADS = 8
FF = 1024
P_SIZE = 128
BX = 1
BY = 2
BZ = 1
LAYERS = 2
NBX = 4
NBY = 32
NBZ = 8


def draw_features(key, part):
    shape = (NBX, NBY, NBZ, P_SIZE, W)
    key_base = jax.random.fold_in(key, 0)
    return jnp.clip(jax.random.normal(key_base, shape, jnp.float32), -6.0, 6.0)


def draw_occupancy(key, part):
    drawn = jax.random.randint(key, (NBX, NBY, NBZ), 1, P_SIZE + 1)
    return drawn.at[0, 0, 0].set(P_SIZE).astype(jnp.int32)


def line_permutation(key, length):
    return jax.random.permutation(key, length)


def draw_dest_bin(key, part):
    lines_x = NBX // BX
    lines_y = NBY // BY
    depth = NBZ // BZ
    count = BX * BY * BZ
    lines = lines_x * lines_y
    key_shift, key_place = jax.random.split(key)
    shifts = jax.vmap(lambda k: line_permutation(k, depth))(jax.random.split(key_shift, lines))
    order = jnp.arange(count, dtype=jnp.int32) % depth
    shift = shifts[:, order]
    place = jax.vmap(lambda k: line_permutation(k, count))(jax.random.split(key_place, lines * depth)).reshape(lines, depth, count)
    source_z = jnp.arange(depth, dtype=jnp.int32)[None, :, None]
    target_z = (source_z + shift[:, None, :]) % depth
    target_local = jnp.take_along_axis(place, target_z, axis=1)
    local_x = target_local // (BY * BZ)
    local_y = target_local // BZ % BY
    local_z = target_local % BZ
    line_x = (jnp.arange(lines, dtype=jnp.int32) // lines_y)[:, None, None]
    line_y = (jnp.arange(lines, dtype=jnp.int32) % lines_y)[:, None, None]
    flat = ((line_x * BX + local_x) * NBY + line_y * BY + local_y) * NBZ + target_z * BZ + local_z
    grid = flat.reshape(lines_x, lines_y, depth, BX, BY, BZ).transpose(0, 3, 1, 4, 2, 5).reshape(NBX, NBY, NBZ)
    return grid.astype(jnp.int32)


def noise(stream_key, shape, scale, reach, kind=jnp.bfloat16):
    return jnp.clip(scale * jax.random.normal(stream_key, shape, jnp.float32), -reach, reach).astype(kind)


def setup_inputs(seed: int = 0) -> dict:
    seeds = jax.random.split(jax.random.key(seed), 12)
    return {
        "features": draw_features(jax.random.fold_in(seeds[11], 71), 0),
        "occupancy": draw_occupancy(jax.random.fold_in(seeds[11], 71), 0),
        "dest_bin": draw_dest_bin(jax.random.fold_in(seeds[11], 71), 0),
        "query_weight": noise(seeds[3], (W, W), W ** -0.5, 0.375),
        "key_weight": noise(seeds[4], (W, W), W ** -0.5, 0.375),
        "value_weight": noise(seeds[5], (W, W), W ** -0.5, 0.375),
        "out_weight": noise(seeds[6], (W, W), W ** -0.5, 0.375),
        "up_weight": noise(seeds[7], (W, FF), W ** -0.5, 0.375),
        "down_weight": noise(seeds[8], (FF, W), FF ** -0.5, 0.1875),
        "attention_gain": jnp.clip(1.0 + 0.15 * jax.random.normal(seeds[9], (W,), jnp.float32), 0.25, 1.75),
        "feed_gain": jnp.clip(1.0 + 0.15 * jax.random.normal(seeds[10], (W,), jnp.float32), 0.25, 1.75),
    }


EPSILON = 1e-05

def layer_norm(values, gain):
    centre = values - lax.optimization_barrier(jnp.mean(values, axis=-1, keepdims=True))
    spread = lax.optimization_barrier(jnp.mean(centre * centre, axis=-1, keepdims=True))
    return centre * lax.rsqrt(spread + EPSILON) * gain

def neighbours(padded):
    parts = [padded[1:-1, 1:-1, 1:-1], padded[:-2, 1:-1, 1:-1], padded[2:, 1:-1, 1:-1], padded[1:-1, :-2, 1:-1], padded[1:-1, 2:, 1:-1], padded[1:-1, 1:-1, :-2], padded[1:-1, 1:-1, 2:]]
    return jnp.stack(parts, axis=3)

def attend(query, keys, values, mask, heads):
    batch, slots, width = query.shape
    head_size = width // heads
    total_keys = keys.shape[1]
    query_heads = query.astype(jnp.float32).reshape(batch, slots, heads, head_size)
    key_heads = keys.astype(jnp.float32).reshape(batch, total_keys, heads, head_size)
    value_heads = values.astype(jnp.float32).reshape(batch, total_keys, heads, head_size)
    scores = jnp.einsum('bqhd,bkhd->bhqk', query_heads, key_heads) * head_size ** (-0.5)
    valid = mask[:, None, None, :]
    scores = jnp.where(valid, scores, -1e+30)
    peak = lax.optimization_barrier(jnp.max(scores, axis=-1, keepdims=True))
    weights = jnp.where(valid, jnp.exp(scores - peak), 0.0)
    weights = (weights / lax.optimization_barrier(jnp.sum(weights, axis=-1, keepdims=True))).astype(jnp.bfloat16)
    mixed = jnp.einsum('bhqk,bkhd->bqhd', weights.astype(jnp.float32), value_heads)
    return mixed.astype(jnp.bfloat16).reshape(batch, slots, width)

def update(rows, attended, occupied, out_weight, up_weight, down_weight, attention_gain, feed_gain):
    batch, slots, width = rows.shape
    mixed = jnp.dot(attended.reshape(-1, width), out_weight, preferred_element_type=jnp.float32)
    hidden = layer_norm(rows.reshape(-1, width) + mixed, attention_gain)
    inner = jax.nn.gelu(jnp.dot(hidden.astype(jnp.bfloat16), up_weight, preferred_element_type=jnp.float32)).astype(jnp.bfloat16)
    grown = jnp.dot(inner, down_weight, preferred_element_type=jnp.float32)
    result = layer_norm(hidden + grown, feed_gain).reshape(batch, slots, width)
    live = jnp.arange(slots, dtype=jnp.int32)[None, :, None] < occupied[:, None, None]
    return jnp.where(live, result, 0.0)

def apply_layer(state, counts, query_weight, key_weight, value_weight, out_weight, up_weight, down_weight, attention_gain, feed_gain):
    grid_x, grid_y, grid_z, slots, width = state.shape
    flat = state.astype(jnp.bfloat16).reshape(-1, width)
    query = jnp.dot(flat, query_weight, preferred_element_type=jnp.float32).astype(jnp.bfloat16).reshape(state.shape)
    keyval = jnp.concatenate([jnp.dot(flat, key_weight, preferred_element_type=jnp.float32), jnp.dot(flat, value_weight, preferred_element_type=jnp.float32)], axis=1)
    keyval = keyval.astype(jnp.bfloat16).reshape(grid_x, grid_y, grid_z, slots, 2 * width)
    padded = jnp.pad(keyval, ((1, 1), (1, 1), (1, 1), (0, 0), (0, 0)))
    padded_counts = jnp.pad(counts, 1)

    def column(index):
        pos_x = (index // grid_y).astype(jnp.int32)
        pos_y = (index % grid_y).astype(jnp.int32)
        zero = jnp.zeros((), jnp.int32)
        block = lax.dynamic_slice(padded, (pos_x, pos_y, zero, zero, zero), (3, 3, grid_z + 2, slots, 2 * width))
        block_counts = lax.dynamic_slice(padded_counts, (pos_x, pos_y, zero), (3, 3, grid_z + 2))
        keys_here = neighbours(block)[0, 0].reshape(grid_z, 7 * slots, 2 * width)
        near = neighbours(block_counts)[0, 0]
        mask = (jnp.arange(slots, dtype=jnp.int32)[None, None, :] < near[:, :, None]).reshape(grid_z, 7 * slots)
        query_here = lax.dynamic_slice(query, (pos_x, pos_y, zero, zero, zero), (1, 1, grid_z, slots, width))[0, 0]
        rows_here = lax.dynamic_slice(state, (pos_x, pos_y, zero, zero, zero), (1, 1, grid_z, slots, width))[0, 0]
        count_here = lax.dynamic_slice(counts, (pos_x, pos_y, zero), (1, 1, grid_z))[0, 0]
        attended = attend(query_here, keys_here[..., :width], keys_here[..., width:], mask, HEADS)
        return update(rows_here, attended, count_here, out_weight, up_weight, down_weight, attention_gain, feed_gain)
    result = lax.map(column, jnp.arange(grid_x * grid_y, dtype=jnp.int32))
    return result.reshape(state.shape)

def migrate(state, counts, dest_bin):
    slots, width = (state.shape[3], state.shape[4])
    targets = dest_bin.reshape(-1).astype(jnp.int32)
    moved = jnp.zeros((targets.shape[0], slots, width), state.dtype).at[targets].set(state.reshape(-1, slots, width))
    moved_counts = jnp.zeros(targets.shape, counts.dtype).at[targets].set(counts.reshape(-1))
    return (moved.reshape(state.shape), moved_counts.reshape(counts.shape))

def reference(features, occupancy, dest_bin, query_weight, key_weight, value_weight, out_weight, up_weight, down_weight, attention_gain, feed_gain):
    state, counts = (features, occupancy)
    for layer in range(LAYERS):
        state = apply_layer(state, counts, query_weight, key_weight, value_weight, out_weight, up_weight, down_weight, attention_gain, feed_gain)
        if layer + 1 < LAYERS:
            state, counts = migrate(state, counts, dest_bin)
    return state
```

```python
import functools
import math

import jax
import jax.numpy as jnp
from jax import lax
from jax.experimental import pallas as pl
from jax.experimental.pallas import tpu as pltpu
from jax.sharding import PartitionSpec as P

MESH = pl.DeviceIdType.MESH
HEADS = 8
EPSILON = 1e-05
SLOTS = 128
WIDTH = 256
HEAD = WIDTH // HEADS
FF = 1024
MARK = 2.0**20
LIMIT = 2.0**19
NEGATIVE = -1e30
SCALE = HEAD**-0.5 * math.log2(math.e)

Y_LOW, Z0_LOW, Z0_HIGH, OWN0, OWN1, Z1_LOW, Z1_HIGH, Y_HIGH, X_FIRST = range(9)
Z_LOW, Z_HIGH = (Z0_LOW, Z1_LOW), (Z0_HIGH, Z1_HIGH)
NEAR = 5 * SLOTS
FAR = 2 * SLOTS
PAIRS = HEADS // 2


def nt(left, right):
    return lax.dot_general(left, right, (((1,), (1,)), ((), ())), preferred_element_type=jnp.float32)


def nn(left, right):
    return jnp.dot(left, right, preferred_element_type=jnp.float32)


def layer_norm(values, gain):
    centre = values - jnp.mean(values, axis=-1, keepdims=True)
    spread = jnp.mean(centre * centre, axis=-1, keepdims=True)
    return centre * lax.rsqrt(spread + EPSILON) * gain


def gelu(x):
    return 0.5 * x * (1.0 + jnp.tanh(math.sqrt(2.0 / math.pi) * (x + 0.044715 * (x * x * x))))


def marked(rows, live):
    return jnp.where(live, rows, MARK).astype(jnp.bfloat16)


def penalty(rows):
    first = (lax.broadcasted_iota(jnp.int32, (8, WIDTH), 1) == 0).astype(jnp.bfloat16)
    return jnp.where(nt(first, rows) > LIMIT, NEGATIVE, 0.0)


def kernel(
    features, occupancy, dest_bin, wq, wk, wv, wo, wu, wd, ga, gf, out,
    state, q_w, k_w, v_w, o_w, u_w, d_w, a_g, f_g,
    rows1, rows2, line, places, q_stack, keys, values, far_keys, far_values,
    near_pen, far_pen, peak, total, mixed, result,
    load_sem, out_sem,
    x_send, x_recv, y_send, y_recv, z_send, z_recv, p_send, p_recv,
    m_send, m_recv, s_send, s_recv,
):
    x, y, z = lax.axis_index("gx"), lax.axis_index("gy"), lax.axis_index("gz")
    nx, ny, nz = lax.axis_size("gx"), lax.axis_size("gy"), lax.axis_size("gz")
    chips = nz // 2
    chip, core = z // 2, z % 2
    twin = (x, y, chip * 2 + (1 - core))

    def around(step):
        return (x, y, lax.rem(z + step, nz))

    def other_chip(step):
        return (x, y, lax.rem(chip + step, chips) * 2 + core)

    has = {
        ("x", 0): x > 0, ("x", 1): x < nx - 1,
        ("y", 0): y > 0, ("y", 1): y < ny - 1,
        ("z", 0): z > 0, ("z", 1): z < nz - 1,
    }
    peer = {
        ("x", 0): (jnp.maximum(x - 1, 0), y, z), ("x", 1): (jnp.minimum(x + 1, nx - 1), y, z),
        ("y", 0): (x, jnp.maximum(y - 1, 0), z), ("y", 1): (x, jnp.minimum(y + 1, ny - 1), z),
        ("z", 0): (x, y, jnp.maximum(z - 1, 0)), ("z", 1): (x, y, jnp.minimum(z + 1, nz - 1)),
    }

    loads = [
        pltpu.make_async_copy(source, target, load_sem.at[i])
        for i, (source, target) in enumerate(
            [
                (features, state), (wq, q_w), (wk, k_w), (wv, v_w), (wo, o_w), (wu, u_w),
                (wd, d_w), (ga, a_g), (gf, f_g),
            ]
        )
    ]
    for load in loads:
        load.start()

    barrier = pltpu.get_barrier_semaphore()
    for step in range(1, nz):
        pl.semaphore_signal(barrier, inc=1, device_id=around(step), device_id_type=MESH)
    for axis in "xy":
        for side in (0, 1):

            @pl.when(has[axis, side])
            def _():
                pl.semaphore_signal(barrier, inc=1, device_id=peer[axis, side], device_id_type=MESH)

    row_id = lax.broadcasted_iota(jnp.int32, (SLOTS, WIDTH), 0)
    tile_row = lax.broadcasted_iota(jnp.int32, (8, 128), 0)
    places[z] = jnp.where(
        tile_row == 0, dest_bin[0], jnp.where(tile_row == 1, dest_bin[1], -1)
    )
    loads[0].wait()
    for b in range(2):
        rows1[OWN0 + b] = marked(state[b], row_id < occupancy[b])

    dead = jnp.full((SLOTS, WIDTH), MARK, jnp.bfloat16)
    for rows in (rows1, rows2):
        for side in (0, 1):

            @pl.when(jnp.logical_not(has["x", side]))
            def _():
                for b in range(2):
                    rows[X_FIRST + 2 * b + side] = dead

            @pl.when(jnp.logical_not(has["y", side]))
            def _():
                rows[(Y_LOW, Y_HIGH)[side]] = dead

    for side in (0, 1):

        @pl.when(jnp.logical_not(has["z", side]))
        def _():
            for b in range(2):
                rows1[(Z_LOW, Z_HIGH)[side][b]] = dead

    greeted = sum((has[axis, side].astype(jnp.int32) for axis in "xy" for side in (0, 1)), nz - 1)
    pl.semaphore_wait(barrier, greeted)

    def x_copy(layer, rows, b, side):
        return pltpu.make_async_remote_copy(
            src_ref=rows.at[OWN0 + b],
            dst_ref=rows.at[X_FIRST + 2 * b + (1 - side)],
            send_sem=x_send.at[layer, b, side],
            recv_sem=x_recv.at[layer, b, 1 - side],
            device_id=peer["x", side],
            device_id_type=MESH,
        )

    def y_copy(layer, rows, side):
        return pltpu.make_async_remote_copy(
            src_ref=rows.at[OWN0 + side],
            dst_ref=rows.at[(Y_LOW, Y_HIGH)[1 - side]],
            send_sem=y_send.at[layer, side],
            recv_sem=y_recv.at[layer, 1 - side],
            device_id=peer["y", side],
            device_id_type=MESH,
        )

    def z_copy(b, side):
        return pltpu.make_async_remote_copy(
            src_ref=rows1.at[OWN0 + b],
            dst_ref=rows1.at[(Z_LOW, Z_HIGH)[1 - side][b]],
            send_sem=z_send.at[b, side],
            recv_sem=z_recv.at[b, 1 - side],
            device_id=peer["z", side],
            device_id_type=MESH,
        )

    def place_copy(step):
        return pltpu.make_async_remote_copy(
            src_ref=places.at[z],
            dst_ref=places.at[z],
            send_sem=p_send.at[step - 1],
            recv_sem=p_recv.at[step - 1],
            device_id=around(step),
            device_id_type=MESH,
        )

    def line_copy(b, step):
        own = line.at[2 * z + b]
        return pltpu.make_async_remote_copy(
            src_ref=own,
            dst_ref=own,
            send_sem=m_send.at[b, step - 1],
            recv_sem=m_recv.at[b, step - 1],
            device_id=other_chip(step),
            device_id_type=MESH,
        )

    def twin_copy(b, step):
        origin = lax.rem(chip - step + chips, chips) * 2 + core
        block = line.at[2 * origin + b]
        return pltpu.make_async_remote_copy(
            src_ref=block,
            dst_ref=block,
            send_sem=s_send.at[b, step],
            recv_sem=s_recv.at[b, step],
            device_id=twin,
            device_id_type=MESH,
        )

    def on(axis, side, act):
        pl.when(has[axis, side])(act)

    for b in range(2):
        for side in (0, 1):
            on("x", side, lambda: x_copy(0, rows1, b, side).start())
        if b == 0:
            for side in (0, 1):
                on("z", side, lambda: z_copy(0, side).start())
                on("z", side, lambda: z_copy(1, side).start())
                on("y", side, lambda: y_copy(0, rows1, side).start())
    for step in range(1, nz):
        place_copy(step).start()
    for load in loads[1:]:
        load.wait()

    lane = lax.broadcasted_iota(jnp.int32, (SLOTS, WIDTH), 1)

    def project(rows, first, count, key_ref, value_ref):
        block = rows[first : first + count].reshape(count * SLOTS, WIDTH)
        key_ref[...] = nn(block, k_w[...]).astype(jnp.bfloat16)
        value_ref[...] = nn(block, v_w[...]).astype(jnp.bfloat16)
        return penalty(block)

    def project_near(rows):
        query = nn(rows[OWN0 : OWN1 + 1].reshape(2 * SLOTS, WIDTH), q_w[...]).astype(jnp.bfloat16)
        for h in range(HEADS):
            inside = (lane >= h * HEAD) & (lane < (h + 1) * HEAD)
            for b in range(2):
                q_stack[b, h * SLOTS : (h + 1) * SLOTS, :] = jnp.where(
                    inside, query[b * SLOTS : (b + 1) * SLOTS], jnp.bfloat16(0.0)
                )
        near_pen[...] = project(rows, 0, 8, keys, values)

    def attend_near(b):
        first = b * 3 * SLOTS
        key = keys.at[first : first + NEAR, :]
        value = values.at[first : first + NEAR, :]
        pen = near_pen[0:1, first : first + NEAR]

        def pair(g, carry):
            here = pl.ds(pl.multiple_of(g * 2 * SLOTS, 2 * SLOTS), 2 * SLOTS)
            scores = nt(q_stack[b, here, :], key[...]) * SCALE + pen
            top = jnp.max(scores, axis=-1, keepdims=True)
            power = jnp.exp2(scores - top)
            peak[b, here, :] = jnp.broadcast_to(top, (2 * SLOTS, 128))
            total[b, here, :] = jnp.broadcast_to(
                jnp.sum(power, axis=-1, keepdims=True), (2 * SLOTS, 128)
            )
            mixed[b, here, :] = nn(power.astype(jnp.bfloat16), value[...])
            return carry

        lax.fori_loop(0, PAIRS, pair, 0)

    def finish(rows, b, previous):
        far_pen[...] = project(rows, X_FIRST + 2 * b, 2, far_keys, far_values)
        pen = far_pen[0:1, :]
        attended = jnp.zeros((SLOTS, WIDTH), jnp.float32)
        for g in range(PAIRS):
            here = slice(g * 2 * SLOTS, (g + 1) * 2 * SLOTS)
            scores = nt(q_stack[b, here, :], far_keys[...]) * SCALE + pen
            old = peak[b, here, :][:, 0:1]
            top = jnp.maximum(jnp.max(scores, axis=-1, keepdims=True), old)
            power = jnp.exp2(scores - top)
            shrink = jnp.exp2(old - top)
            whole = total[b, here, :][:, 0:1] * shrink + jnp.sum(power, axis=-1, keepdims=True)
            both = mixed[b, here, :] * shrink + nn(power.astype(jnp.bfloat16), far_values[...])
            both = both / whole
            for i in range(2):
                h = 2 * g + i
                inside = (lane >= h * HEAD) & (lane < (h + 1) * HEAD)
                attended = jnp.where(inside, both[i * SLOTS : (i + 1) * SLOTS], attended)
        hidden = layer_norm(previous + nn(attended.astype(jnp.bfloat16), o_w[...]), a_g[...])
        inner = gelu(nn(hidden.astype(jnp.bfloat16), u_w[...])).astype(jnp.bfloat16)
        return layer_norm(hidden + nn(inner, d_w[...]), f_g[...])

    for side in (0, 1):
        for b in range(2):
            on("z", 1 - side, lambda: z_copy(b, side).wait_recv())
        on("y", 1 - side, lambda: y_copy(0, rows1, side).wait_recv())
    project_near(rows1)
    for b in range(2):
        attend_near(b)

    for step in range(1, nz):
        place_copy(step).wait_recv()
    wide = (nz, 8, 128)
    source_id = 2 * lax.broadcasted_iota(jnp.int32, wide, 0) + lax.broadcasted_iota(jnp.int32, wide, 1)
    table = places[...]

    def source(z_at, b):
        flat = (x * (2 * ny) + 2 * y + b) * nz + z_at
        found = jnp.max(jnp.where(table == flat, source_id, 0))
        return jnp.clip(found, 0, 2 * nz - 1)

    z_below, z_above = jnp.maximum(z - 1, 0), jnp.minimum(z + 1, nz - 1)
    origin = [[source(at, b) for b in range(2)] for at in (z_below, z, z_above)]

    for b in range(2):
        for side in (0, 1):
            on("x", 1 - side, lambda: x_copy(0, rows1, b, side).wait_recv())
        updated = finish(rows1, b, state[b])
        line[2 * z + b] = marked(updated, row_id < occupancy[b])
        for step in range(1, chips):
            line_copy(b, step).start()
        twin_copy(b, 0).start()

    for b in range(2):
        for step in range(1, chips):
            line_copy(b, step).wait_recv()
            twin_copy(b, step).start()
    for b in range(2):
        for step in range(chips):
            twin_copy(b, step).wait_recv()

    for b in range(2):
        rows2[OWN0 + b] = line[origin[1][b]]
        for side in (0, 1):
            on("x", side, lambda: x_copy(1, rows2, b, side).start())
    for side in (0, 1):
        on("y", side, lambda: y_copy(1, rows2, side).start())
    for b in range(2):
        for side, at in ((0, 0), (1, 2)):
            slot = (Z_LOW, Z_HIGH)[side][b]
            rows2[slot] = jnp.where(has["z", side], line[origin[at][b]], dead)
    for side in (0, 1):
        on("y", 1 - side, lambda: y_copy(1, rows2, side).wait_recv())
    project_near(rows2)
    for b in range(2):
        attend_near(b)
    for b in range(2):
        for side in (0, 1):
            on("x", 1 - side, lambda: x_copy(1, rows2, b, side).wait_recv())
        own = rows2[OWN0 + b].astype(jnp.float32)
        result[b] = jnp.where(own < LIMIT, finish(rows2, b, own), 0.0)
        pltpu.make_async_copy(result.at[b], out.at[b], out_sem.at[b]).start()

    for side in (0, 1):
        for b in range(2):
            on("x", side, lambda: x_copy(0, rows1, b, side).wait_send())
            on("x", side, lambda: x_copy(1, rows2, b, side).wait_send())
            on("z", side, lambda: z_copy(b, side).wait_send())
        on("y", side, lambda: y_copy(0, rows1, side).wait_send())
        on("y", side, lambda: y_copy(1, rows2, side).wait_send())
    for step in range(1, nz):
        place_copy(step).wait_send()
    for b in range(2):
        for step in range(1, chips):
            line_copy(b, step).wait_send()
        for step in range(chips):
            twin_copy(b, step).wait_send()
        pltpu.make_async_copy(result.at[b], out.at[b], out_sem.at[b]).wait()


def shards(features, occupancy, dest_bin, wq, wk, wv, wo, wu, wd, ga, gf):
    nz = lax.axis_size("gz")
    bf16, f32 = jnp.bfloat16, jnp.float32
    dma = pltpu.SemaphoreType.DMA
    block = (SLOTS, WIDTH)
    anywhere, smem = pl.BlockSpec(memory_space=pl.ANY), pl.BlockSpec(memory_space=pltpu.SMEM)
    out = pl.pallas_call(
        kernel,
        out_shape=jax.ShapeDtypeStruct((2, *block), f32),
        in_specs=[anywhere, smem, smem] + [anywhere] * 8,
        out_specs=anywhere,
        scratch_shapes=[
            pltpu.VMEM((2, *block), f32),
            *[pltpu.VMEM((WIDTH, WIDTH), bf16)] * 4,
            pltpu.VMEM((WIDTH, FF), bf16),
            pltpu.VMEM((FF, WIDTH), bf16),
            pltpu.VMEM((1, WIDTH), f32),
            pltpu.VMEM((1, WIDTH), f32),
            pltpu.VMEM((12, *block), bf16),
            pltpu.VMEM((12, *block), bf16),
            pltpu.VMEM((2 * nz, *block), bf16),
            pltpu.VMEM((nz, 8, 128), jnp.int32),
            pltpu.VMEM((2, HEADS * SLOTS, WIDTH), bf16),
            pltpu.VMEM((8 * SLOTS, WIDTH), bf16),
            pltpu.VMEM((8 * SLOTS, WIDTH), bf16),
            pltpu.VMEM((FAR, WIDTH), bf16),
            pltpu.VMEM((FAR, WIDTH), bf16),
            pltpu.VMEM((8, 8 * SLOTS), f32),
            pltpu.VMEM((8, FAR), f32),
            pltpu.VMEM((2, HEADS * SLOTS, 128), f32),
            pltpu.VMEM((2, HEADS * SLOTS, 128), f32),
            pltpu.VMEM((2, HEADS * SLOTS, WIDTH), f32),
            pltpu.VMEM((2, *block), f32),
            dma((9,)),
            dma((2,)),
            dma((2, 2, 2)),
            dma((2, 2, 2)),
            dma((2, 2)),
            dma((2, 2)),
            dma((2, 2)),
            dma((2, 2)),
            dma((nz - 1,)),
            dma((nz - 1,)),
            dma((2, nz // 2 - 1)),
            dma((2, nz // 2 - 1)),
            dma((2, nz // 2)),
            dma((2, nz // 2)),
        ],
        compiler_params=pltpu.CompilerParams(
            collective_id=0, has_side_effects=True, vmem_limit_bytes=60 << 20
        ),
        name="evolve",
    )(
        features.reshape(2, *block),
        occupancy.reshape(2),
        dest_bin.reshape(2),
        wq, wk, wv, wo, wu, wd,
        ga.reshape(1, WIDTH),
        gf.reshape(1, WIDTH),
    )
    return out.reshape(features.shape)


def solution(mesh):
    cells = P("gx", "gy", "gz")
    return jax.shard_map(
        shards,
        mesh=mesh,
        in_specs=(P("gx", "gy", "gz", None, None), cells, cells) + (P(),) * 8,
        out_specs=P("gx", "gy", "gz", None, None),
        check_vma=False,
    )
```

```python
import functools
import math

import jax
import jax.numpy as jnp
from jax import lax
from jax.experimental import pallas as pl
from jax.experimental.pallas import tpu as pltpu
from jax.sharding import PartitionSpec as P

MESH = pl.DeviceIdType.MESH
HEADS = 8
EPSILON = 1e-05
SLOTS = 128
WIDTH = 256
HEAD = WIDTH // HEADS
FF = 1024
MARK = 2.0**20
LIMIT = 2.0**19
NEGATIVE = -1e30
SCALE = HEAD**-0.5 * math.log2(math.e)

Y_LOW, Z0_LOW, Z0_HIGH, OWN0, OWN1, Z1_LOW, Z1_HIGH, Y_HIGH, X_FIRST = range(9)
Z_LOW, Z_HIGH = (Z0_LOW, Z1_LOW), (Z0_HIGH, Z1_HIGH)
NEAR = 5 * SLOTS
PAIRS = HEADS // 2
UNROLL = 4
RELAY = True
HALF = SLOTS // 2
PIECES = ((0, 0), (0, 1), (1, 0), (1, 1))


def nt(left, right):
    return lax.dot_general(left, right, (((1,), (1,)), ((), ())), preferred_element_type=jnp.float32)


def nn(left, right):
    return jnp.dot(left, right, preferred_element_type=jnp.float32)


def layer_norm(values, gain):
    centre = values - jnp.mean(values, axis=-1, keepdims=True)
    spread = jnp.mean(centre * centre, axis=-1, keepdims=True)
    return centre * lax.rsqrt(spread + EPSILON) * gain


def gelu(x):
    return 0.5 * x * (1.0 + jnp.tanh(math.sqrt(2.0 / math.pi) * (x + 0.044715 * (x * x * x))))


def marked(rows, live):
    return jnp.where(live, rows, MARK).astype(jnp.bfloat16)


def penalty(rows):
    return jnp.where(rows[:, :SLOTS].astype(jnp.float32) > LIMIT, NEGATIVE, 0.0)


def twice(columns):
    return jnp.concatenate([columns, columns], axis=1)


def kernel(
    features, occupancy, dest_bin, wq, wk, wv, wo, wu, wd, ga, gf, out,
    state, q_w, k_w, v_w, o_w, u_w, d_w, a_g, f_g,
    rows1, rows2, line_low, line_high, places, qt_w, vt_w, q_stack, keys, values, near_pen, peak, total, mixed, result,
    load_sem, out_sem,
    x_send, x_recv, y_send, y_recv, z_send, z_recv, p_send, p_recv,
    m_send, m_recv, r_send, s_send, s_recv,
):
    x, y, z = lax.axis_index("gx"), lax.axis_index("gy"), lax.axis_index("gz")
    nx, ny, nz = lax.axis_size("gx"), lax.axis_size("gy"), lax.axis_size("gz")
    chips = nz // 2
    line = (line_low, line_high)
    chip, core = z // 2, z % 2
    twin = (x, y, chip * 2 + (1 - core))

    def around(step):
        return (x, y, lax.rem(z + step, nz))

    def other_chip(step):
        return (x, y, lax.rem(chip + step, chips) * 2 + core)

    has = {
        ("x", 0): x > 0, ("x", 1): x < nx - 1,
        ("y", 0): y > 0, ("y", 1): y < ny - 1,
        ("z", 0): z > 0, ("z", 1): z < nz - 1,
    }
    peer = {
        ("x", 0): (jnp.maximum(x - 1, 0), y, z), ("x", 1): (jnp.minimum(x + 1, nx - 1), y, z),
        ("y", 0): (x, jnp.maximum(y - 1, 0), z), ("y", 1): (x, jnp.minimum(y + 1, ny - 1), z),
        ("z", 0): (x, y, jnp.maximum(z - 1, 0)), ("z", 1): (x, y, jnp.minimum(z + 1, nz - 1)),
    }

    loads = [
        pltpu.make_async_copy(source, target, load_sem.at[i])
        for i, (source, target) in enumerate(
            [
                (features, state), (wq, q_w), (wk, k_w), (wv, v_w), (wo, o_w), (wu, u_w),
                (wd, d_w), (ga, a_g), (gf, f_g),
            ]
        )
    ]
    for load in loads:
        load.start()

    barrier = pltpu.get_barrier_semaphore()
    for step in range(1, nz):
        pl.semaphore_signal(barrier, inc=1, device_id=around(step), device_id_type=MESH)
    for axis in "xy":
        for side in (0, 1):

            @pl.when(has[axis, side])
            def _():
                pl.semaphore_signal(barrier, inc=1, device_id=peer[axis, side], device_id_type=MESH)

    row_id = lax.broadcasted_iota(jnp.int32, (SLOTS, WIDTH), 0)
    tile_row = lax.broadcasted_iota(jnp.int32, (8, 128), 0)
    places[z] = jnp.where(
        tile_row == 0, dest_bin[0], jnp.where(tile_row == 1, dest_bin[1], -1)
    )
    loads[0].wait()
    for b in range(2):
        rows1[OWN0 + b] = marked(state[b], row_id < occupancy[b])

    dead = jnp.full((SLOTS, WIDTH), MARK, jnp.bfloat16)
    for rows in (rows1, rows2):
        for side in (0, 1):

            @pl.when(jnp.logical_not(has["y", side]))
            def _():
                rows[(Y_LOW, Y_HIGH)[side]] = dead

    for side in (0, 1):

        @pl.when(jnp.logical_not(has["z", side]))
        def _():
            for b in range(2):
                rows1[(Z_LOW, Z_HIGH)[side][b]] = dead

    greeted = sum((has[axis, side].astype(jnp.int32) for axis in "xy" for side in (0, 1)), nz - 1)
    pl.semaphore_wait(barrier, greeted)

    def x_copy(rows, b, side, half=None):
        span = slice(0, SLOTS) if half is None else slice(half * HALF, (half + 1) * HALF)
        number = 0 if half is None else 1 + half
        return pltpu.make_async_remote_copy(
            src_ref=rows.at[OWN0 + b, span],
            dst_ref=rows.at[X_FIRST + 2 * b + (1 - side), span],
            send_sem=x_send.at[number, b, side],
            recv_sem=x_recv.at[number, b, 1 - side],
            device_id=peer["x", side],
            device_id_type=MESH,
        )

    def y_copy(layer, rows, side):
        return pltpu.make_async_remote_copy(
            src_ref=rows.at[OWN0 + side],
            dst_ref=rows.at[(Y_LOW, Y_HIGH)[1 - side]],
            send_sem=y_send.at[layer, side],
            recv_sem=y_recv.at[layer, 1 - side],
            device_id=peer["y", side],
            device_id_type=MESH,
        )

    def z_copy(b, side):
        return pltpu.make_async_remote_copy(
            src_ref=rows1.at[OWN0 + b],
            dst_ref=rows1.at[(Z_LOW, Z_HIGH)[1 - side][b]],
            send_sem=z_send.at[b, side],
            recv_sem=z_recv.at[b, 1 - side],
            device_id=peer["z", side],
            device_id_type=MESH,
        )

    def place_copy(step):
        return pltpu.make_async_remote_copy(
            src_ref=places.at[z],
            dst_ref=places.at[z],
            send_sem=p_send.at[step - 1],
            recv_sem=p_recv.at[step - 1],
            device_id=around(step),
            device_id_type=MESH,
        )

    def part(origin, piece):
        b, half = PIECES[piece]
        return line[half].at[2 * origin + b]

    def line_copy(piece, step):
        own = part(z, piece)
        return pltpu.make_async_remote_copy(
            src_ref=own,
            dst_ref=own,
            send_sem=m_send.at[piece, step - 1],
            recv_sem=m_recv.at[piece, step - 1],
            device_id=other_chip(step),
            device_id_type=MESH,
        )

    def relay_copy(piece):
        block = part(lax.rem(chip + 2, chips) * 2 + core, piece)
        upward = chip == 2
        return pltpu.make_async_remote_copy(
            src_ref=block,
            dst_ref=block,
            send_sem=r_send.at[piece],
            recv_sem=m_recv.at[piece, jnp.where(upward, 2, 0)],
            device_id=(x, y, jnp.where(upward, 6, 0) + core),
            device_id_type=MESH,
        )

    def twin_copy(piece, step):
        block = part(lax.rem(chip - step + chips, chips) * 2 + core, piece)
        return pltpu.make_async_remote_copy(
            src_ref=block,
            dst_ref=block,
            send_sem=s_send.at[piece, step],
            recv_sem=s_recv.at[piece, step],
            device_id=twin,
            device_id_type=MESH,
        )

    inner_chip = (chip == 1) | (chip == 2)

    def direct(step, act):
        if step == 2 or not RELAY:
            act()
        else:
            pl.when(chip != (3 if step == 1 else 0))(act)

    def share(piece):
        for step in (2, 1, 3):
            direct(step, lambda: line_copy(piece, step).start())
        twin_copy(piece, 0).start()

    def pass_on(piece):
        line_copy(piece, 2).wait_recv()
        if RELAY:
            pl.when(inner_chip)(lambda: relay_copy(piece).start())
        twin_copy(piece, 2).start()
        for step in (1, 3):
            line_copy(piece, step).wait_recv()
            twin_copy(piece, step).start()

    def arrived(piece):
        for step in range(chips):
            twin_copy(piece, step).wait_recv()

    def on(axis, side, act):
        pl.when(has[axis, side])(act)

    for side in (0, 1):
        on("x", side, lambda: x_copy(rows1, 0, side).start())
    for side in (0, 1):
        for b in range(2):
            on("z", side, lambda: z_copy(b, side).start())
        on("y", side, lambda: y_copy(0, rows1, side).start())
    for step in range(1, nz):
        place_copy(step).start()
    for load in loads[1:]:
        load.wait()

    qt_w[...] = q_w[...].astype(jnp.float32).T.astype(jnp.bfloat16)
    vt_w[...] = v_w[...].astype(jnp.float32).T.astype(jnp.bfloat16)
    for b in range(2):
        q_stack[b] = jnp.zeros((WIDTH, HEADS * SLOTS), jnp.bfloat16)

    def project(rows, first, count):
        block = rows[first : first + count].reshape(count * SLOTS, WIDTH)
        key = nn(block, k_w[...]).astype(jnp.bfloat16)
        value = nt(vt_w[...], block).astype(jnp.bfloat16)
        return key, value, penalty(block)

    def project_near(rows):
        query = nt(qt_w[...], rows[OWN0 : OWN1 + 1].reshape(2 * SLOTS, WIDTH)).astype(jnp.bfloat16)
        for b in range(2):
            for h in range(HEADS):
                down, across = slice(h * HEAD, (h + 1) * HEAD), slice(h * SLOTS, (h + 1) * SLOTS)
                q_stack[b, down, across] = query[down, b * SLOTS : (b + 1) * SLOTS]
        keys[...], values[...], near_pen[...] = project(rows, 0, 8)

    def attend_near(b):
        near = slice(b * 3 * SLOTS, b * 3 * SLOTS + NEAR)

        def pair(g, carry):
            across = pl.ds(pl.multiple_of(g * 2 * SLOTS, 2 * SLOTS), 2 * SLOTS)
            down = pl.ds(pl.multiple_of(g * 2 * HEAD, 2 * HEAD), 2 * HEAD)
            scores = nn(keys[near, :], q_stack[b, :, across]) * SCALE + twice(near_pen[near, :])
            top = jnp.max(scores, axis=0, keepdims=True)
            power = jnp.exp2(scores - top)
            peak[b, g] = top
            total[b, g] = jnp.sum(power, axis=0, keepdims=True)
            both = nn(values[down, near], power.astype(jnp.bfloat16))
            mixed[b, g] = jnp.concatenate([both[:HEAD, :SLOTS], both[HEAD:, SLOTS:]], axis=0)
            return carry

        lax.fori_loop(0, PAIRS, pair, 0, unroll=UNROLL)

    def absorb(rows, b, side):
        key, value, pen = project(rows, X_FIRST + 2 * b + side, 1)
        pen = twice(pen)
        for g in range(PAIRS):
            scores = nn(key, q_stack[b, :, g * 2 * SLOTS : (g + 1) * 2 * SLOTS]) * SCALE + pen
            old = peak[b, g]
            top = jnp.maximum(jnp.max(scores, axis=0, keepdims=True), old)
            power = jnp.exp2(scores - top)
            shrink = jnp.exp2(old - top)
            peak[b, g] = top
            total[b, g] = total[b, g] * shrink + jnp.sum(power, axis=0, keepdims=True)
            both = nn(value[g * 2 * HEAD : (g + 1) * 2 * HEAD, :], power.astype(jnp.bfloat16))
            for i in range(2):
                down, across = slice(i * HEAD, (i + 1) * HEAD), slice(i * SLOTS, (i + 1) * SLOTS)
                mixed[b, g, down, :] = mixed[b, g, down, :] * shrink[:, across] + both[down, across]

    def attended(b):
        pieces = []
        for g in range(PAIRS):
            whole = 1.0 / total[b, g]
            for i in range(2):
                piece = mixed[b, g, i * HEAD : (i + 1) * HEAD, :]
                pieces.append(piece * whole[:, i * SLOTS : (i + 1) * SLOTS])
        return jnp.concatenate(pieces, axis=0)

    def feed(heads, previous):
        weighed = nn(heads.T.astype(jnp.bfloat16), o_w[...])
        hidden = layer_norm(previous + weighed, a_g[...])
        inner = gelu(nn(hidden.astype(jnp.bfloat16), u_w[...])).astype(jnp.bfloat16)
        return layer_norm(hidden + nn(inner, d_w[...]), f_g[...])

    for side in (0, 1):
        for b in range(2):
            on("z", 1 - side, lambda: z_copy(b, side).wait_recv())
        on("y", 1 - side, lambda: y_copy(0, rows1, side).wait_recv())
    project_near(rows1)
    for side in (0, 1):

        @pl.when(has["x", side])
        def _():
            x_copy(rows1, 0, side).wait_send()
            x_copy(rows1, 1, side).start()

    for b in range(2):
        attend_near(b)

    for step in range(1, nz):
        place_copy(step).wait_recv()
    wide = (nz, 8, 128)
    source_id = 2 * lax.broadcasted_iota(jnp.int32, wide, 0) + lax.broadcasted_iota(jnp.int32, wide, 1)
    table = places[...]

    def source(z_at, b):
        flat = (x * (2 * ny) + 2 * y + b) * nz + z_at
        found = jnp.max(jnp.where(table == flat, source_id, 0))
        return jnp.clip(found, 0, 2 * nz - 1)

    z_below, z_above = jnp.maximum(z - 1, 0), jnp.minimum(z + 1, nz - 1)
    origin = [[source(at, b) for b in range(2)] for at in (z_below, z, z_above)]

    for b in range(2):
        for side in (0, 1):

            @pl.when(has["x", side])
            def _():
                x_copy(rows1, b, 1 - side).wait_recv()
                absorb(rows1, b, side)

        updated = feed(attended(b), state[b])
        sent = marked(updated, row_id < occupancy[b])
        for half in range(2):
            line[half][2 * z + b] = sent[half * HALF : (half + 1) * HALF]
            share(2 * b + half)

    pass_on(0)
    pass_on(1)
    pass_on(2)
    arrived(0)
    arrived(2)
    for half in range(2):
        if half == 1:
            pass_on(3)
            arrived(1)
            arrived(3)
        span = slice(half * HALF, (half + 1) * HALF)
        for b in range(2):
            rows2[OWN0 + b, span] = line[half][origin[1][b]]
        for side in (0, 1):

            @pl.when(has["x", side])
            def _():
                for b in range(2):
                    if half == 1:
                        x_copy(rows2, b, side, 0).wait_send()
                    x_copy(rows2, b, side, half).start()

    for side in (0, 1):
        on("y", side, lambda: y_copy(1, rows2, side).start())
    for b in range(2):
        for side, at in ((0, 0), (1, 2)):
            slot = (Z_LOW, Z_HIGH)[side][b]
            for half in range(2):
                span = slice(half * HALF, (half + 1) * HALF)
                rows2[slot, span] = jnp.where(has["z", side], line[half][origin[at][b]], dead[:HALF])
    for side in (0, 1):
        on("y", 1 - side, lambda: y_copy(1, rows2, side).wait_recv())
    project_near(rows2)
    for b in range(2):
        attend_near(b)
    for b in range(2):
        for side in (0, 1):

            @pl.when(has["x", side])
            def _():
                for half in range(2):
                    x_copy(rows2, b, 1 - side, half).wait_recv()
                absorb(rows2, b, side)

    own = rows2[OWN0 : OWN1 + 1].reshape(2 * SLOTS, WIDTH).astype(jnp.float32)
    final = feed(jnp.concatenate([attended(0), attended(1)], axis=1), own)
    result[...] = jnp.where(own < LIMIT, final, 0.0)
    result_copy = pltpu.make_async_copy(result, out, out_sem)
    result_copy.start()

    for side in (0, 1):
        on("x", side, lambda: x_copy(rows1, 1, side).wait_send())
        for b in range(2):
            on("x", side, lambda: x_copy(rows2, b, side, 1).wait_send())
            on("z", side, lambda: z_copy(b, side).wait_send())
        on("y", side, lambda: y_copy(0, rows1, side).wait_send())
        on("y", side, lambda: y_copy(1, rows2, side).wait_send())
    for step in range(1, nz):
        place_copy(step).wait_send()
    for piece in range(len(PIECES)):
        for step in range(1, chips):
            direct(step, lambda: line_copy(piece, step).wait_send())
        if RELAY:
            pl.when(inner_chip)(lambda: relay_copy(piece).wait_send())
        for step in range(chips):
            twin_copy(piece, step).wait_send()
    result_copy.wait()


def shards(features, occupancy, dest_bin, wq, wk, wv, wo, wu, wd, ga, gf):
    nz = lax.axis_size("gz")
    bf16, f32 = jnp.bfloat16, jnp.float32
    dma = pltpu.SemaphoreType.DMA
    block = (SLOTS, WIDTH)
    anywhere, smem = pl.BlockSpec(memory_space=pl.ANY), pl.BlockSpec(memory_space=pltpu.SMEM)
    out = pl.pallas_call(
        kernel,
        out_shape=jax.ShapeDtypeStruct((2 * SLOTS, WIDTH), f32),
        in_specs=[anywhere, smem, smem] + [anywhere] * 8,
        out_specs=anywhere,
        scratch_shapes=[
            pltpu.VMEM((2, *block), f32),
            *[pltpu.VMEM((WIDTH, WIDTH), bf16)] * 4,
            pltpu.VMEM((WIDTH, FF), bf16),
            pltpu.VMEM((FF, WIDTH), bf16),
            pltpu.VMEM((1, WIDTH), f32),
            pltpu.VMEM((1, WIDTH), f32),
            pltpu.VMEM((12, *block), bf16),
            pltpu.VMEM((12, *block), bf16),
            pltpu.VMEM((2 * nz, HALF, WIDTH), bf16),
            pltpu.VMEM((2 * nz, HALF, WIDTH), bf16),
            pltpu.VMEM((nz, 8, 128), jnp.int32),
            pltpu.VMEM((WIDTH, WIDTH), bf16),
            pltpu.VMEM((WIDTH, WIDTH), bf16),
            pltpu.VMEM((2, WIDTH, HEADS * SLOTS), bf16),
            pltpu.VMEM((8 * SLOTS, WIDTH), bf16),
            pltpu.VMEM((WIDTH, 8 * SLOTS), bf16),
            pltpu.VMEM((8 * SLOTS, SLOTS), f32),
            pltpu.VMEM((2, PAIRS, 1, 2 * SLOTS), f32),
            pltpu.VMEM((2, PAIRS, 1, 2 * SLOTS), f32),
            pltpu.VMEM((2, PAIRS, 2 * HEAD, SLOTS), f32),
            pltpu.VMEM((2 * SLOTS, WIDTH), f32),
            dma((9,)),
            dma,
            dma((3, 2, 2)),
            dma((3, 2, 2)),
            dma((2, 2)),
            dma((2, 2)),
            dma((2, 2)),
            dma((2, 2)),
            dma((nz - 1,)),
            dma((nz - 1,)),
            dma((len(PIECES), nz // 2 - 1)),
            dma((len(PIECES), nz // 2 - 1)),
            dma((len(PIECES),)),
            dma((len(PIECES), nz // 2)),
            dma((len(PIECES), nz // 2)),
        ],
        compiler_params=pltpu.CompilerParams(
            collective_id=0, has_side_effects=True, vmem_limit_bytes=60 << 20
        ),
        name="evolve",
    )(
        features.reshape(2, *block),
        occupancy.reshape(2),
        dest_bin.reshape(2),
        wq, wk, wv, wo, wu, wd,
        ga.reshape(1, WIDTH),
        gf.reshape(1, WIDTH),
    )
    return out.reshape(features.shape)


def solution(mesh):
    cells = P("gx", "gy", "gz")
    return jax.shard_map(
        shards,
        mesh=mesh,
        in_specs=(P("gx", "gy", "gz", None, None), cells, cells) + (P(),) * 8,
        out_specs=P("gx", "gy", "gz", None, None),
        check_vma=False,
    )
```

```python
import functools
import math

import jax
import jax.numpy as jnp
from jax import lax
from jax.experimental import pallas as pl
from jax.experimental.pallas import tpu as pltpu
from jax.sharding import PartitionSpec as P

MESH = pl.DeviceIdType.MESH
HEADS = 8
EPSILON = 1e-05
SLOTS = 128
WIDTH = 256
HEAD = WIDTH // HEADS
FF = 1024
MARK = 2.0**20
LIMIT = 2.0**19
NEGATIVE = -1e30
SCALE = HEAD**-0.5 * math.log2(math.e)

Y_LOW, Z0_LOW, Z0_HIGH, OWN0, OWN1, Z1_LOW, Z1_HIGH, Y_HIGH, X_FIRST = range(9)
Z_LOW, Z_HIGH = (Z0_LOW, Z1_LOW), (Z0_HIGH, Z1_HIGH)
NEAR = 5 * SLOTS
PAIRS = HEADS // 2
UNROLL = 4
RELAY = True
HALF = SLOTS // 2
PIECES = ((0, 0), (0, 1), (1, 0), (1, 1))


def nt(left, right):
    return lax.dot_general(left, right, (((1,), (1,)), ((), ())), preferred_element_type=jnp.float32)


def nn(left, right):
    return jnp.dot(left, right, preferred_element_type=jnp.float32)


def layer_norm(values, gain):
    centre = values - jnp.mean(values, axis=-1, keepdims=True)
    spread = jnp.mean(centre * centre, axis=-1, keepdims=True)
    return centre * lax.rsqrt(spread + EPSILON) * gain


def gelu(x):
    return 0.5 * x * (1.0 + jnp.tanh(math.sqrt(2.0 / math.pi) * (x + 0.044715 * (x * x * x))))


def marked(rows, live):
    return jnp.where(live, rows, MARK).astype(jnp.bfloat16)


def penalty(rows):
    return jnp.where(rows[:, :SLOTS].astype(jnp.float32) > LIMIT, NEGATIVE, 0.0)


def twice(columns):
    return jnp.concatenate([columns, columns], axis=1)


def kernel(
    features, occupancy, dest_bin, wq, wk, wv, wo, wu, wd, ga, gf, out,
    state, q_w, k_w, v_w, o_w, u_w, d_w, a_g, f_g,
    rows1, rows2, line_low, line_high, places, qt_w, vt_w, q_stack, keys, values, near_pen, peak, total, mixed, result,
    load_sem, out_sem,
    x_send, x_recv, y_send, y_recv, z_send, z_recv, p_send, p_recv,
    m_send, m_recv, r_send, s_send, s_recv,
):
    x, y, z = lax.axis_index("gx"), lax.axis_index("gy"), lax.axis_index("gz")
    nx, ny, nz = lax.axis_size("gx"), lax.axis_size("gy"), lax.axis_size("gz")
    chips = nz // 2
    line = (line_low, line_high)
    chip, core = z // 2, z % 2
    twin = (x, y, chip * 2 + (1 - core))

    def around(step):
        return (x, y, lax.rem(z + step, nz))

    def other_chip(step):
        return (x, y, lax.rem(chip + step, chips) * 2 + core)

    has = {
        ("x", 0): x > 0, ("x", 1): x < nx - 1,
        ("y", 0): y > 0, ("y", 1): y < ny - 1,
        ("z", 0): z > 0, ("z", 1): z < nz - 1,
    }
    peer = {
        ("x", 0): (jnp.maximum(x - 1, 0), y, z), ("x", 1): (jnp.minimum(x + 1, nx - 1), y, z),
        ("y", 0): (x, jnp.maximum(y - 1, 0), z), ("y", 1): (x, jnp.minimum(y + 1, ny - 1), z),
        ("z", 0): (x, y, jnp.maximum(z - 1, 0)), ("z", 1): (x, y, jnp.minimum(z + 1, nz - 1)),
    }

    loads = [
        pltpu.make_async_copy(source, target, load_sem.at[i])
        for i, (source, target) in enumerate(
            [
                (features, state), (wq, q_w), (wk, k_w), (wv, v_w), (wo, o_w), (wu, u_w),
                (wd, d_w), (ga, a_g), (gf, f_g),
            ]
        )
    ]
    for load in loads:
        load.start()

    barrier = pltpu.get_barrier_semaphore()
    for step in range(1, nz):
        pl.semaphore_signal(barrier, inc=1, device_id=around(step), device_id_type=MESH)
    for axis in "xy":
        for side in (0, 1):

            @pl.when(has[axis, side])
            def _():
                pl.semaphore_signal(barrier, inc=1, device_id=peer[axis, side], device_id_type=MESH)

    row_id = lax.broadcasted_iota(jnp.int32, (SLOTS, WIDTH), 0)
    tile_row = lax.broadcasted_iota(jnp.int32, (8, 128), 0)
    places[z] = jnp.where(
        tile_row == 0, dest_bin[0], jnp.where(tile_row == 1, dest_bin[1], -1)
    )
    loads[0].wait()
    for b in range(2):
        rows1[OWN0 + b] = marked(state[b], row_id < occupancy[b])

    dead = jnp.full((SLOTS, WIDTH), MARK, jnp.bfloat16)
    for rows in (rows1, rows2):
        for side in (0, 1):

            @pl.when(jnp.logical_not(has["y", side]))
            def _():
                rows[(Y_LOW, Y_HIGH)[side]] = dead

    for side in (0, 1):

        @pl.when(jnp.logical_not(has["z", side]))
        def _():
            for b in range(2):
                rows1[(Z_LOW, Z_HIGH)[side][b]] = dead

    greeted = sum((has[axis, side].astype(jnp.int32) for axis in "xy" for side in (0, 1)), nz - 1)
    pl.semaphore_wait(barrier, greeted)

    def x_copy(rows, b, side, half=None):
        span = slice(0, SLOTS) if half is None else slice(half * HALF, (half + 1) * HALF)
        number = 0 if half is None else 1 + half
        return pltpu.make_async_remote_copy(
            src_ref=rows.at[OWN0 + b, span],
            dst_ref=rows.at[X_FIRST + 2 * b + (1 - side), span],
            send_sem=x_send.at[number, b, side],
            recv_sem=x_recv.at[number, b, 1 - side],
            device_id=peer["x", side],
            device_id_type=MESH,
        )

    def y_copy(layer, rows, side):
        return pltpu.make_async_remote_copy(
            src_ref=rows.at[OWN0 + side],
            dst_ref=rows.at[(Y_LOW, Y_HIGH)[1 - side]],
            send_sem=y_send.at[layer, side],
            recv_sem=y_recv.at[layer, 1 - side],
            device_id=peer["y", side],
            device_id_type=MESH,
        )

    def z_copy(b, side):
        return pltpu.make_async_remote_copy(
            src_ref=rows1.at[OWN0 + b],
            dst_ref=rows1.at[(Z_LOW, Z_HIGH)[1 - side][b]],
            send_sem=z_send.at[b, side],
            recv_sem=z_recv.at[b, 1 - side],
            device_id=peer["z", side],
            device_id_type=MESH,
        )

    def place_copy(step):
        return pltpu.make_async_remote_copy(
            src_ref=places.at[z],
            dst_ref=places.at[z],
            send_sem=p_send.at[step - 1],
            recv_sem=p_recv.at[step - 1],
            device_id=around(step),
            device_id_type=MESH,
        )

    def part(origin, piece):
        b, half = PIECES[piece]
        return line[half].at[2 * origin + b]

    def line_copy(piece, step):
        own = part(z, piece)
        return pltpu.make_async_remote_copy(
            src_ref=own,
            dst_ref=own,
            send_sem=m_send.at[piece, step - 1],
            recv_sem=m_recv.at[piece, step - 1],
            device_id=other_chip(step),
            device_id_type=MESH,
        )

    def relay_copy(piece):
        block = part(lax.rem(chip + 2, chips) * 2 + core, piece)
        upward = chip == 2
        return pltpu.make_async_remote_copy(
            src_ref=block,
            dst_ref=block,
            send_sem=r_send.at[piece],
            recv_sem=m_recv.at[piece, jnp.where(upward, 2, 0)],
            device_id=(x, y, jnp.where(upward, 6, 0) + core),
            device_id_type=MESH,
        )

    def twin_copy(piece, step):
        block = part(lax.rem(chip - step + chips, chips) * 2 + core, piece)
        return pltpu.make_async_remote_copy(
            src_ref=block,
            dst_ref=block,
            send_sem=s_send.at[piece, step],
            recv_sem=s_recv.at[piece, step],
            device_id=twin,
            device_id_type=MESH,
        )

    inner_chip = (chip == 1) | (chip == 2)

    def direct(step, act):
        if step == 2 or not RELAY:
            act()
        else:
            pl.when(chip != (3 if step == 1 else 0))(act)

    def share(piece):
        for step in (2, 1, 3):
            direct(step, lambda: line_copy(piece, step).start())
        twin_copy(piece, 0).start()

    def pass_on(piece):
        line_copy(piece, 2).wait_recv()
        if RELAY:
            pl.when(inner_chip)(lambda: relay_copy(piece).start())
        twin_copy(piece, 2).start()
        for step in (1, 3):
            line_copy(piece, step).wait_recv()
            twin_copy(piece, step).start()

    def arrived(piece):
        for step in range(chips):
            twin_copy(piece, step).wait_recv()

    def on(axis, side, act):
        pl.when(has[axis, side])(act)

    for side in (0, 1):
        on("x", side, lambda: x_copy(rows1, 0, side).start())
    for side in (0, 1):
        for b in range(2):
            on("z", side, lambda: z_copy(b, side).start())
        on("y", side, lambda: y_copy(0, rows1, side).start())
    for step in range(1, nz):
        place_copy(step).start()
    for load in loads[1:]:
        load.wait()

    qt_w[...] = q_w[...].astype(jnp.float32).T.astype(jnp.bfloat16)
    vt_w[...] = v_w[...].astype(jnp.float32).T.astype(jnp.bfloat16)
    for b in range(2):
        q_stack[b] = jnp.zeros((WIDTH, HEADS * SLOTS), jnp.bfloat16)

    def project(rows, first, count):
        block = rows[first : first + count].reshape(count * SLOTS, WIDTH)
        key = nn(block, k_w[...]).astype(jnp.bfloat16)
        value = nt(vt_w[...], block).astype(jnp.bfloat16)
        return key, value, penalty(block)

    def project_near(rows):
        query = nt(qt_w[...], rows[OWN0 : OWN1 + 1].reshape(2 * SLOTS, WIDTH)).astype(jnp.bfloat16)
        for b in range(2):
            for h in range(HEADS):
                down, across = slice(h * HEAD, (h + 1) * HEAD), slice(h * SLOTS, (h + 1) * SLOTS)
                q_stack[b, down, across] = query[down, b * SLOTS : (b + 1) * SLOTS]
        keys[...], values[...], near_pen[...] = project(rows, 0, 8)

    def attend_near(b):
        near = slice(b * 3 * SLOTS, b * 3 * SLOTS + NEAR)

        def pair(g, carry):
            across = pl.ds(pl.multiple_of(g * 2 * SLOTS, 2 * SLOTS), 2 * SLOTS)
            down = pl.ds(pl.multiple_of(g * 2 * HEAD, 2 * HEAD), 2 * HEAD)
            scores = nn(keys[near, :], q_stack[b, :, across]) * SCALE + twice(near_pen[near, :])
            top = jnp.max(scores, axis=0, keepdims=True)
            power = jnp.exp2(scores - top)
            peak[b, g] = top
            total[b, g] = jnp.sum(power, axis=0, keepdims=True)
            both = nn(values[down, near], power.astype(jnp.bfloat16))
            mixed[b, g] = jnp.concatenate([both[:HEAD, :SLOTS], both[HEAD:, SLOTS:]], axis=0)
            return carry

        lax.fori_loop(0, PAIRS, pair, 0, unroll=UNROLL)

    def absorb(rows, b, side):
        key, value, pen = project(rows, X_FIRST + 2 * b + side, 1)
        pen = twice(pen)
        for g in range(PAIRS):
            scores = nn(key, q_stack[b, :, g * 2 * SLOTS : (g + 1) * 2 * SLOTS]) * SCALE + pen
            old = peak[b, g]
            top = jnp.maximum(jnp.max(scores, axis=0, keepdims=True), old)
            power = jnp.exp2(scores - top)
            shrink = jnp.exp2(old - top)
            peak[b, g] = top
            total[b, g] = total[b, g] * shrink + jnp.sum(power, axis=0, keepdims=True)
            both = nn(value[g * 2 * HEAD : (g + 1) * 2 * HEAD, :], power.astype(jnp.bfloat16))
            for i in range(2):
                down, across = slice(i * HEAD, (i + 1) * HEAD), slice(i * SLOTS, (i + 1) * SLOTS)
                mixed[b, g, down, :] = mixed[b, g, down, :] * shrink[:, across] + both[down, across]

    def attended(b):
        pieces = []
        for g in range(PAIRS):
            whole = 1.0 / total[b, g]
            for i in range(2):
                piece = mixed[b, g, i * HEAD : (i + 1) * HEAD, :]
                pieces.append(piece * whole[:, i * SLOTS : (i + 1) * SLOTS])
        return jnp.concatenate(pieces, axis=0)

    def feed(heads, previous):
        weighed = nn(heads.T.astype(jnp.bfloat16), o_w[...])
        hidden = layer_norm(previous + weighed, a_g[...])
        inner = gelu(nn(hidden.astype(jnp.bfloat16), u_w[...])).astype(jnp.bfloat16)
        return layer_norm(hidden + nn(inner, d_w[...]), f_g[...])

    for side in (0, 1):
        for b in range(2):
            on("z", 1 - side, lambda: z_copy(b, side).wait_recv())
        on("y", 1 - side, lambda: y_copy(0, rows1, side).wait_recv())
    project_near(rows1)
    for side in (0, 1):

        @pl.when(has["x", side])
        def _():
            x_copy(rows1, 0, side).wait_send()
            x_copy(rows1, 1, side).start()

    for b in range(2):
        attend_near(b)

    for step in range(1, nz):
        place_copy(step).wait_recv()
    wide = (nz, 8, 128)
    source_id = 2 * lax.broadcasted_iota(jnp.int32, wide, 0) + lax.broadcasted_iota(jnp.int32, wide, 1)
    table = places[...]

    def source(z_at, b):
        flat = (x * (2 * ny) + 2 * y + b) * nz + z_at
        found = jnp.max(jnp.where(table == flat, source_id, 0))
        return jnp.clip(found, 0, 2 * nz - 1)

    z_below, z_above = jnp.maximum(z - 1, 0), jnp.minimum(z + 1, nz - 1)
    origin = [[source(at, b) for b in range(2)] for at in (z_below, z, z_above)]

    for b in range(2):
        for side in (0, 1):

            @pl.when(has["x", side])
            def _():
                x_copy(rows1, b, 1 - side).wait_recv()
                absorb(rows1, b, side)

        if b == 1:
            pass_on(0)
            pass_on(1)
        updated = feed(attended(b), state[b])
        sent = marked(updated, row_id < occupancy[b])
        for half in range(2):
            line[half][2 * z + b] = sent[half * HALF : (half + 1) * HALF]
            share(2 * b + half)

    pass_on(2)
    arrived(0)
    arrived(2)
    for half in range(2):
        if half == 1:
            pass_on(3)
            arrived(1)
            arrived(3)
        span = slice(half * HALF, (half + 1) * HALF)
        for b in range(2):
            rows2[OWN0 + b, span] = line[half][origin[1][b]]
        for side in (0, 1):

            @pl.when(has["x", side])
            def _():
                for b in range(2):
                    if half == 1:
                        x_copy(rows2, b, side, 0).wait_send()
                    x_copy(rows2, b, side, half).start()

    for side in (0, 1):
        on("y", side, lambda: y_copy(1, rows2, side).start())
    for b in range(2):
        for side, at in ((0, 0), (1, 2)):
            slot = (Z_LOW, Z_HIGH)[side][b]
            for half in range(2):
                span = slice(half * HALF, (half + 1) * HALF)
                rows2[slot, span] = jnp.where(has["z", side], line[half][origin[at][b]], dead[:HALF])
    for side in (0, 1):
        on("y", 1 - side, lambda: y_copy(1, rows2, side).wait_recv())
    project_near(rows2)
    for b in range(2):
        attend_near(b)
    for b in range(2):
        for side in (0, 1):

            @pl.when(has["x", side])
            def _():
                for half in range(2):
                    x_copy(rows2, b, 1 - side, half).wait_recv()
                absorb(rows2, b, side)

    own = rows2[OWN0 : OWN1 + 1].reshape(2 * SLOTS, WIDTH).astype(jnp.float32)
    final = feed(jnp.concatenate([attended(0), attended(1)], axis=1), own)
    result[...] = jnp.where(own < LIMIT, final, 0.0)
    result_copy = pltpu.make_async_copy(result, out, out_sem)
    result_copy.start()

    for side in (0, 1):
        on("x", side, lambda: x_copy(rows1, 1, side).wait_send())
        for b in range(2):
            on("x", side, lambda: x_copy(rows2, b, side, 1).wait_send())
            on("z", side, lambda: z_copy(b, side).wait_send())
        on("y", side, lambda: y_copy(0, rows1, side).wait_send())
        on("y", side, lambda: y_copy(1, rows2, side).wait_send())
    for step in range(1, nz):
        place_copy(step).wait_send()
    for piece in range(len(PIECES)):
        for step in range(1, chips):
            direct(step, lambda: line_copy(piece, step).wait_send())
        if RELAY:
            pl.when(inner_chip)(lambda: relay_copy(piece).wait_send())
        for step in range(chips):
            twin_copy(piece, step).wait_send()
    result_copy.wait()


def shards(features, occupancy, dest_bin, wq, wk, wv, wo, wu, wd, ga, gf):
    nz = lax.axis_size("gz")
    bf16, f32 = jnp.bfloat16, jnp.float32
    dma = pltpu.SemaphoreType.DMA
    block = (SLOTS, WIDTH)
    anywhere, smem = pl.BlockSpec(memory_space=pl.ANY), pl.BlockSpec(memory_space=pltpu.SMEM)
    out = pl.pallas_call(
        kernel,
        out_shape=jax.ShapeDtypeStruct((2 * SLOTS, WIDTH), f32),
        in_specs=[anywhere, smem, smem] + [anywhere] * 8,
        out_specs=anywhere,
        scratch_shapes=[
            pltpu.VMEM((2, *block), f32),
            *[pltpu.VMEM((WIDTH, WIDTH), bf16)] * 4,
            pltpu.VMEM((WIDTH, FF), bf16),
            pltpu.VMEM((FF, WIDTH), bf16),
            pltpu.VMEM((1, WIDTH), f32),
            pltpu.VMEM((1, WIDTH), f32),
            pltpu.VMEM((12, *block), bf16),
            pltpu.VMEM((12, *block), bf16),
            pltpu.VMEM((2 * nz, HALF, WIDTH), bf16),
            pltpu.VMEM((2 * nz, HALF, WIDTH), bf16),
            pltpu.VMEM((nz, 8, 128), jnp.int32),
            pltpu.VMEM((WIDTH, WIDTH), bf16),
            pltpu.VMEM((WIDTH, WIDTH), bf16),
            pltpu.VMEM((2, WIDTH, HEADS * SLOTS), bf16),
            pltpu.VMEM((8 * SLOTS, WIDTH), bf16),
            pltpu.VMEM((WIDTH, 8 * SLOTS), bf16),
            pltpu.VMEM((8 * SLOTS, SLOTS), f32),
            pltpu.VMEM((2, PAIRS, 1, 2 * SLOTS), f32),
            pltpu.VMEM((2, PAIRS, 1, 2 * SLOTS), f32),
            pltpu.VMEM((2, PAIRS, 2 * HEAD, SLOTS), f32),
            pltpu.VMEM((2 * SLOTS, WIDTH), f32),
            dma((9,)),
            dma,
            dma((3, 2, 2)),
            dma((3, 2, 2)),
            dma((2, 2)),
            dma((2, 2)),
            dma((2, 2)),
            dma((2, 2)),
            dma((nz - 1,)),
            dma((nz - 1,)),
            dma((len(PIECES), nz // 2 - 1)),
            dma((len(PIECES), nz // 2 - 1)),
            dma((len(PIECES),)),
            dma((len(PIECES), nz // 2)),
            dma((len(PIECES), nz // 2)),
        ],
        compiler_params=pltpu.CompilerParams(
            collective_id=0, has_side_effects=True, vmem_limit_bytes=60 << 20
        ),
        name="evolve",
    )(
        features.reshape(2, *block),
        occupancy.reshape(2),
        dest_bin.reshape(2),
        wq, wk, wv, wo, wu, wd,
        ga.reshape(1, WIDTH),
        gf.reshape(1, WIDTH),
    )
    return out.reshape(features.shape)


def solution(mesh):
    cells = P("gx", "gy", "gz")
    return jax.shard_map(
        shards,
        mesh=mesh,
        in_specs=(P("gx", "gy", "gz", None, None), cells, cells) + (P(),) * 8,
        out_specs=P("gx", "gy", "gz", None, None),
        check_vma=False,
    )
```
